32 devices in a mesh: dp: 16 (over z, y, x), tensor: 2 (over core).
Axes of the slice: x: 2, y: 2, z: 4, core: 2. Of those that a mesh axis runs over, the one named last changes fastest.
Arguments:
- tokens: bfloat16 [32768, 768], P('dp'), may hold values from -6 to 6
- lengths: int32 [64], P('dp'), may hold values from 64 to 512, as said below
- projections: bfloat16 [3, 768, 768], P(None, None, 'tensor'), may hold values from -0.21875 to 0.21875
- attention_bias: float32 [2, 768], P(None, 'tensor'), may hold values from -3 to 3
- output_weight: bfloat16 [768, 768], P('tensor'), may hold values from -1.75 to 1.75
- output_bias: float32 [768], replicated, may hold values from -3 to 3
- first_gain: float32 [768], replicated, may hold values from 0.4 to 1.6
- first_shift: float32 [768], replicated, may hold values from -3 to 3
- inner_weight: bfloat16 [768, 3072], P(None, 'tensor'), may hold values from -0.21875 to 0.21875
- inner_bias: float32 [3072], P('tensor'), may hold values from -3 to 3
- outer_weight: bfloat16 [3072, 768], P('tensor'), may hold values from -0.21875 to 0.21875
- outer_bias: float32 [768], replicated, may hold values from -3 to 3
- second_gain: float32 [768], replicated, may hold values from 0.4 to 1.6
- second_shift: float32 [768], replicated, may hold values from -3 to 3
- cotangent: bfloat16 [32768, 768], P('dp'), may hold values from -6 to 6
Outputs:
- layer_output: bfloat16 [32768, 768], P('dp')
- input_gradient: bfloat16 [32768, 768], P('dp')
- projections_gradient: float32 [3, 768, 768], P(None, None, 'tensor')
- attention_bias_gradient: float32 [2, 768], P(None, 'tensor')
- output_weight_gradient: float32 [768, 768], P('tensor')
- output_bias_gradient: float32 [768], replicated
- first_gain_gradient: float32 [768], replicated
- first_shift_gradient: float32 [768], replicated
- inner_weight_gradient: float32 [768, 3072], P(None, 'tensor')
- inner_bias_gradient: float32 [3072], P('tensor')
- outer_weight_gradient: float32 [3072, 768], P('tensor')
- outer_bias_gradient: float32 [768], replicated
- second_gain_gradient: float32 [768], replicated
- second_shift_gradient: float32 [768], replicated
The draws below stay inside these ranges and needn't reach their ends.
Inputs may be any that keep to these rules, and one draw needn't show every extreme that they name: `lengths`: each sequence has 64 to 512 live tokens; one sequence has exactly 512.
All inputs are finite; a program needn't handle non-finite values.
Results may differ from the reference program's by a relative error of at most 0.023.
Values may be sent and summed in bfloat16 or wider, within the bound.
A program may use at most 192 MiB of HBM per device.

```python
import jax
import jax.numpy as jnp
from jax import lax

D = 768
FF = 3072
HEAD = 64
SEQ_LEN = 512
SLOTS = 4
SEQS = 64
TOKENS = 32768
N_DP = 16
N_TENSOR = 2


def draw_lengths(key, part):
    first_key, second_key = jax.random.split(jax.random.fold_in(key, 17))
    values = jax.random.randint(first_key, (SEQS,), SEQ_LEN // 8, SEQ_LEN + 1)
    chosen = jax.random.randint(second_key, (), 0, SEQS)
    return jnp.where(jnp.arange(SEQS) == chosen, SEQ_LEN, values).astype(jnp.int32)


def block_scale(rng, dims, shards, smallest, high):
    factor_of = 1.0
    for position, blocks in shards:
        steps = jax.random.uniform(jax.random.fold_in(jax.random.fold_in(rng, 6), position), (blocks,), jnp.float32, smallest / len(shards), high / len(shards))
        factor_of = factor_of * jnp.repeat(jnp.exp(steps), dims[position] // blocks).reshape((-1,) + (1,) * (len(dims) - 1 - position))
    return factor_of


def gaussian(own_key, extent, width, most, cuts=(), kind=jnp.bfloat16):
    gain = block_scale(own_key, extent, cuts, -0.22, 0.18) if cuts else 1.0
    values = jax.random.normal(own_key, extent, jnp.float32) * width * gain
    return jnp.minimum(jnp.maximum(values, -most), most).astype(kind)


def setup_inputs(seed: int = 0) -> dict:
    keys = jax.random.split(jax.random.key(seed), 16)
    return {
        "tokens": gaussian(keys[0], (TOKENS, D), 1.0, 6.0, ((0, 16),)),
        "lengths": draw_lengths(jax.random.fold_in(keys[15], 71), 0),
        "projections": gaussian(keys[2], (3, D, D), D ** -0.5, 0.21875, ((2, 2),)),
        "attention_bias": gaussian(keys[3], (2, D), 0.5, 3.0, ((1, 2),), jnp.float32),
        "output_weight": gaussian(keys[4], (D, D), (D // HEAD) ** -0.5, 1.75, ((0, 2),)),
        "output_bias": gaussian(keys[5], (D,), 0.5, 3.0, (), jnp.float32),
        "first_gain": jnp.clip(1.0 + 0.12 * jax.random.normal(keys[6], (D,), jnp.float32), 0.4, 1.6),
        "first_shift": gaussian(keys[7], (D,), 0.4, 3.0, (), jnp.float32),
        "inner_weight": gaussian(keys[8], (D, FF), D ** -0.5, 0.21875, ((1, 2),)),
        "inner_bias": gaussian(keys[9], (FF,), 0.5, 3.0, ((0, 2),), jnp.float32),
        "outer_weight": gaussian(keys[10], (FF, D), (FF // 4) ** -0.5, 0.21875, ((0, 2),)),
        "outer_bias": gaussian(keys[11], (D,), 0.5, 3.0, (), jnp.float32),
        "second_gain": jnp.clip(1.0 + 0.12 * jax.random.normal(keys[12], (D,), jnp.float32), 0.4, 1.6),
        "second_shift": gaussian(keys[13], (D,), 0.4, 3.0, (), jnp.float32),
        "cotangent": gaussian(keys[14], (TOKENS, D), 1.0, 6.0, ((0, 16),)),
    }


@jax.custom_vjp
def low(v):
    return lax.optimization_barrier(v.astype(jnp.bfloat16)).astype(jnp.float32)

@jax.custom_vjp
def low_back(v):
    return v

def low_keep(v):
    return (low(v), None)

def low_pass(kept, grad):
    return (grad,)

def back_keep(v):
    return (v, None)

def back_low(kept, grad):
    return (low(grad),)
low.defvjp(low_keep, low_pass)
low_back.defvjp(back_keep, back_low)

def matmul(left, right):
    return jnp.dot(left, right, precision=lax.Precision.HIGHEST)

def normalize(values, gain_vector, shift_vector):
    centered = values - lax.optimization_barrier(jnp.mean(values, axis=-1, keepdims=True))
    variance = lax.optimization_barrier(jnp.mean(centered * centered, axis=-1, keepdims=True))
    return centered * lax.rsqrt(variance + 1e-06) * gain_vector + shift_vector

def layer(inputs, visible, projections, attention_bias, output_weight, output_bias, first_gain, first_shift, inner_weight, inner_bias, outer_weight, outer_bias, second_gain, second_shift):
    slot_count = visible.shape[0]
    row_count = inputs.shape[0]
    group_width = D // N_TENSOR
    group_hidden = FF // N_TENSOR
    group_heads = group_width // HEAD
    shaped = (slot_count, SEQ_LEN, group_heads, HEAD)
    inputs_low = low(inputs)
    attention = jnp.zeros((row_count, D), jnp.float32)
    for member in range(N_TENSOR):
        columns = slice(member * group_width, (member + 1) * group_width)
        shared = low_back(inputs_low)
        queries = low_back(low(matmul(shared, projections[0][:, columns]) + attention_bias[0][columns]))
        keys_all = low_back(low(matmul(shared, projections[1][:, columns])))
        values_all = low_back(low(matmul(shared, projections[2][:, columns]) + attention_bias[1][columns]))
        scores = jnp.einsum('sqhd,skhd->shqk', queries.reshape(shaped), keys_all.reshape(shaped), precision=lax.Precision.HIGHEST)
        scores = low_back(scores * HEAD ** (-0.5))
        scores = jnp.where(visible[:, None, None, :], scores, -1e+30)
        weights_soft = jax.nn.softmax(scores, axis=-1)
        mixed = jnp.einsum('shqk,skhd->sqhd', low(weights_soft), values_all.reshape(shaped), precision=lax.Precision.HIGHEST)
        mixed = low_back(low(mixed.reshape(row_count, group_width)))
        attention = attention + low(matmul(mixed, output_weight[columns]))
    first_sum = inputs + low_back(attention) + output_bias
    first_out = normalize(first_sum, first_gain, first_shift)
    first_low = low(first_out)
    feedforward = jnp.zeros((row_count, D), jnp.float32)
    for member in range(N_TENSOR):
        hidden_cols = slice(member * group_hidden, (member + 1) * group_hidden)
        shared = low_back(first_low)
        before = low_back(matmul(shared, inner_weight[:, hidden_cols]) + inner_bias[hidden_cols])
        after = low(jax.nn.gelu(before, approximate=False))
        feedforward = feedforward + low(matmul(after, outer_weight[hidden_cols]))
    second_sum = first_out + low_back(feedforward) + outer_bias
    return normalize(second_sum, second_gain, second_shift)

def reference(tokens, lengths, projections, attention_bias, output_weight, output_bias, first_gain, first_shift, inner_weight, inner_bias, outer_weight, outer_bias, second_gain, second_shift, cotangent):
    params = tuple((a.astype(jnp.float32) for a in (projections, attention_bias, output_weight, output_bias, first_gain, first_shift, inner_weight, inner_bias, outer_weight, outer_bias, second_gain, second_shift)))
    groups = tokens.astype(jnp.float32).reshape(N_DP, SLOTS * SEQ_LEN, D)
    upstream = cotangent.astype(jnp.float32).reshape(N_DP, SLOTS * SEQ_LEN, D)
    group_lengths = lengths.astype(jnp.int32).reshape(N_DP, SLOTS)

    def accumulate(carried, entry):
        inputs, lengths_group, grad_group = entry
        visible = jnp.arange(SEQ_LEN, dtype=jnp.int32)[None, :] < lengths_group[:, None]

        def forward(inputs_value, *weights):
            return layer(inputs_value, visible, *weights)
        result, pullback = jax.vjp(forward, inputs, *params)
        grads = pullback(grad_group)
        summed = tuple((c + g for c, g in zip(carried, grads[1:])))
        return (summed, (result.astype(jnp.bfloat16), grads[0].astype(jnp.bfloat16)))
    initial = tuple((jnp.zeros_like(p) for p in params))
    summed, (outputs, input_grads) = lax.scan(accumulate, initial, (groups, group_lengths, upstream))
    return (outputs.reshape(TOKENS, D), input_grads.reshape(TOKENS, D), summed[0], summed[1], summed[2], summed[3], summed[4], summed[5], summed[6], summed[7], summed[8], summed[9], summed[10], summed[11])
```

```python
import functools

import jax
import jax.numpy as jnp
from jax import lax
from jax.experimental import pallas as pl
from jax.experimental.pallas import tpu as pltpu
from jax.sharding import PartitionSpec as P

HEAD = 64
PAIR = 2 * HEAD
SCALE = HEAD ** (-0.5)
F32 = jnp.float32
BF16 = jnp.bfloat16


def dot(left, right, dims):
    return lax.dot_general(left, right, (dims, ((), ())), preferred_element_type=F32)


def scores_of(keys_block, queries, length):
    scores = dot(keys_block, queries * SCALE, ((1,), (1,)))
    slot = lax.broadcasted_iota(jnp.int32, scores.shape, 0)
    return jnp.where(slot < length, scores, -1e30)


def attend_kernel(length_ref, q_ref, k_ref, v_ref, o_ref, l_ref):
    length = length_ref[pl.program_id(0)]
    mixed = []
    for h in range(2):
        cols = slice(h * HEAD, (h + 1) * HEAD)
        scores = scores_of(k_ref[:, cols], q_ref[:, cols], length)
        top = jnp.max(scores, axis=0, keepdims=True)
        exponent = jnp.exp(scores - top)
        total = jnp.sum(exponent, axis=0, keepdims=True)
        weights = (exponent * (1.0 / total)).astype(BF16)
        mixed.append(dot(v_ref[:, cols], weights, ((0,), (0,))))
        l_ref[0, 0, h : h + 1, :] = top + jnp.log(total)
    o_ref[...] = jnp.concatenate(mixed, axis=0).T.astype(BF16)


def attend_back_kernel(length_ref, q_ref, k_ref, v_ref, g_ref, l_ref, dq_ref, dk_ref, dv_ref):
    length = length_ref[pl.program_id(0)]
    dq, dk, dv = [], [], []
    for h in range(2):
        cols = slice(h * HEAD, (h + 1) * HEAD)
        q, k, v, g = q_ref[:, cols], k_ref[:, cols], v_ref[:, cols], g_ref[:, cols]
        weights = jnp.exp(scores_of(k, q, length) - l_ref[0, 0, h : h + 1, :])
        grad_weights = dot(v, g, ((1,), (1,)))
        centre = jnp.sum(weights * grad_weights, axis=0, keepdims=True)
        grad_scores = (weights * (grad_weights - centre)).astype(BF16)
        dq.append(dot(k, grad_scores, ((0,), (0,))))
        dk.append(dot(grad_scores, q, ((1,), (0,))))
        dv.append(dot(weights.astype(BF16), g, ((1,), (0,))))
    dq_ref[...] = (jnp.concatenate(dq, axis=0) * SCALE).T.astype(BF16)
    dk_ref[...] = (jnp.concatenate(dk, axis=1) * SCALE).astype(BF16)
    dv_ref[...] = jnp.concatenate(dv, axis=1).astype(BF16)


def attention_call(kernel, lengths, arrays, logs, outs, flops):
    count = lengths.shape[0]
    rows, width = arrays[0].shape
    span = rows // count
    block = pl.BlockSpec((span, PAIR), lambda s, p, n: (s, p))
    log_block = pl.BlockSpec((1, 1, 2, span), lambda s, p, n: (s, p, 0, 0))
    log_shape = jax.ShapeDtypeStruct((count, width // PAIR, 2, span), F32)
    out_shape = [jax.ShapeDtypeStruct((rows, width), BF16)] * outs
    out_specs = [block] * outs
    if not logs:
        out_shape.append(log_shape)
        out_specs.append(log_block)
    return pl.pallas_call(
        kernel,
        grid_spec=pltpu.PrefetchScalarGridSpec(
            num_scalar_prefetch=1,
            grid=(count, width // PAIR),
            in_specs=[block] * len(arrays) + [log_block] * len(logs),
            out_specs=out_specs,
        ),
        out_shape=out_shape,
        compiler_params=pltpu.CompilerParams(vmem_limit_bytes=40 * 1024 * 1024),
        cost_estimate=pl.CostEstimate(
            flops=flops * rows * span * width * 8,
            bytes_accessed=2 * rows * width * (len(arrays) + outs),
            transcendentals=rows * span * width // HEAD,
        ),
    )(lengths, *arrays, *logs)


def layer_norm(values, gain_vector, shift_vector):
    centered = values - jnp.mean(values, axis=-1, keepdims=True)
    variance = jnp.mean(centered * centered, axis=-1, keepdims=True)
    inverse = lax.rsqrt(variance + 1e-06)
    normed = centered * inverse
    return (normed * gain_vector + shift_vector, normed, inverse)


def norm_backward(upstream, normed, inverse, gain_vector):
    scaled = upstream * gain_vector
    return inverse * (
        scaled
        - jnp.mean(scaled, axis=-1, keepdims=True)
        - normed * jnp.mean(scaled * normed, axis=-1, keepdims=True)
    )


def swap(array):
    return lax.ppermute(array, "tensor", [(0, 1), (1, 0)])


def reduce_part(part, order, size):
    me = lax.axis_index("dp")
    for bit in order:
        pairs = [(i, i ^ (1 << bit)) for i in range(size)]
        half = part.shape[0] // 2
        mine = (me >> bit) & 1
        sent = lax.dynamic_slice_in_dim(part, (1 - mine) * half, half, 0)
        kept = lax.dynamic_slice_in_dim(part, mine * half, half, 0)
        part = (kept.astype(F32) + lax.ppermute(sent, "dp", pairs).astype(F32)).astype(BF16)
    for bit in reversed(order):
        pairs = [(i, i ^ (1 << bit)) for i in range(size)]
        other = lax.ppermute(part, "dp", pairs)
        first = ((me >> bit) & 1) == 0
        part = jnp.concatenate(
            [jnp.where(first, part, other), jnp.where(first, other, part)], axis=0
        )
    return part


def reduce_rows(block, size):
    bits = size.bit_length() - 1
    ways = 3
    rows = block.shape[0]
    share = -(-rows // (ways * size)) * size
    if share * ways != rows:
        block = jnp.pad(block, ((0, share * ways - rows), (0, 0)))
    done = []
    for way in range(ways):
        order = [(way + step) % bits for step in range(bits)]
        done.append(reduce_part(block[way * share : (way + 1) * share], order, size))
    return jnp.concatenate(done, axis=0)[:rows]


def per_device(
    size,
    tokens,
    lengths,
    projections,
    attention_bias,
    output_weight,
    output_bias,
    first_gain,
    first_shift,
    inner_weight,
    inner_bias,
    outer_weight,
    outer_bias,
    second_gain,
    second_shift,
    cotangent,
):
    side = lax.axis_index("tensor")
    rows = tokens.shape[0] // 2
    slots = lengths.shape[0] // 2
    width = tokens.shape[1]
    local = projections.shape[2]
    hidden = inner_weight.shape[1]
    tokens = lax.dynamic_slice_in_dim(tokens, side * rows, rows, 0)
    cotangent = lax.dynamic_slice_in_dim(cotangent, side * rows, rows, 0)
    lengths = lax.dynamic_slice_in_dim(lengths, side * slots, slots, 0)

    proj = (projections, swap(projections))
    small = jnp.concatenate([attention_bias[0], attention_bias[1], inner_bias])
    smalls = (small, swap(small))
    out_w = (output_weight, swap(output_weight))
    inner_w = (inner_weight, swap(inner_weight))
    outer_w = (outer_weight, swap(outer_weight))

    inputs = tokens.astype(F32)
    saved = []
    attention = output_bias
    for g in range(2):
        q_bias, v_bias = smalls[g][:local], smalls[g][local : 2 * local]
        q = (dot(tokens, proj[g][0], ((1,), (0,))) + q_bias).astype(BF16)
        k = dot(tokens, proj[g][1], ((1,), (0,))).astype(BF16)
        v = (dot(tokens, proj[g][2], ((1,), (0,))) + v_bias).astype(BF16)
        mixed, logs = attention_call(attend_kernel, lengths, (q, k, v), (), 1, 1)
        attention = attention + dot(mixed, out_w[g], ((1,), (0,)))
        saved.append((q, k, v, mixed, logs))
    first_out, first_normed, first_inverse = layer_norm(
        inputs + attention, first_gain, first_shift
    )
    first_low = first_out.astype(BF16)
    hiddens = []
    feedforward = outer_bias
    for g in range(2):
        before = dot(first_low, inner_w[g], ((1,), (0,))) + smalls[g][2 * local :]
        cdf = 0.5 * (1.0 + lax.erf(before * (0.5**0.5)))
        after = (before * cdf).astype(BF16)
        slope = cdf + before * (jnp.exp(-0.5 * before * before) * 0.3989422804014327)
        after, slope = lax.optimization_barrier((after, slope.astype(BF16)))
        hiddens.append((after, slope))
        feedforward = feedforward + dot(after, outer_w[g], ((1,), (0,)))
    layer_output, second_normed, second_inverse = layer_norm(
        first_out + feedforward, second_gain, second_shift
    )
    layer_output = lax.all_gather(layer_output.astype(BF16), "tensor", axis=0, tiled=True)
    upstream = cotangent.astype(F32)
    second_gain_gradient = jnp.sum(upstream * second_normed, axis=0)
    second_shift_gradient = jnp.sum(upstream, axis=0)
    grad_second = norm_backward(upstream, second_normed, second_inverse, second_gain)
    outer_bias_gradient = jnp.sum(grad_second, axis=0)
    grad_second_low = grad_second.astype(BF16)

    inner_g, outer_g, inner_bias_g = [None] * 2, [None] * 2, [None] * 2
    grad_first_out = grad_second
    for g in (1, 0):
        after, slope = hiddens[g]
        grad_after = dot(grad_second_low, outer_w[g], ((1,), (1,)))
        grad_before = (grad_after * slope.astype(F32)).astype(BF16)
        outer_g[g] = dot(after, grad_second_low, ((0,), (0,))).astype(BF16)
        inner_g[g] = dot(first_low, grad_before, ((0,), (0,))).astype(BF16)
        inner_bias_g[g] = jnp.sum(grad_before.astype(F32), axis=0)
        grad_first_out = grad_first_out + dot(grad_before, inner_w[g], ((1,), (1,)))

    def pair_sum(own, other):
        return (own.astype(F32) + swap(other).astype(F32)).astype(BF16)

    outer_sum = pair_sum(outer_g[0], outer_g[1])
    inner_sum = pair_sum(inner_g[0], inner_g[1])
    columns = range(0, hidden, width)
    ffn = reduce_rows(
        jnp.concatenate([inner_sum[:, c : c + width] for c in columns] + [outer_sum], axis=0), size
    )
    inner_weight_gradient = jnp.concatenate(
        [ffn[i * width : (i + 1) * width] for i in range(len(columns))], axis=1
    ).astype(F32)
    outer_weight_gradient = ffn[len(columns) * width :].astype(F32)

    first_gain_gradient = jnp.sum(grad_first_out * first_normed, axis=0)
    first_shift_gradient = jnp.sum(grad_first_out, axis=0)
    grad_first = norm_backward(grad_first_out, first_normed, first_inverse, first_gain)
    output_bias_gradient = jnp.sum(grad_first, axis=0)
    grad_first_low = grad_first.astype(BF16)
    grad_inputs = grad_first
    packed, group_bias = [None] * 2, [None] * 2
    for g in (1, 0):
        q, k, v, mixed, logs = saved[g]
        out_g = dot(mixed, grad_first_low, ((0,), (0,)))
        grad_mixed = dot(grad_first_low, out_w[g], ((1,), (1,))).astype(BF16)
        grads = attention_call(attend_back_kernel, lengths, (q, k, v, grad_mixed), (logs,), 3, 3)
        proj_g = [dot(tokens, grad, ((0,), (0,))) for grad in grads]
        out_halves = [out_g[:, c : c + local] for c in range(0, width, local)]
        group_bias[g] = [
            jnp.sum(grads[0].astype(F32), axis=0),
            jnp.sum(grads[2].astype(F32), axis=0),
            inner_bias_g[g],
        ]
        vectors = jnp.concatenate(
            group_bias[g]
            + [
                output_bias_gradient,
                first_gain_gradient,
                first_shift_gradient,
                outer_bias_gradient,
                second_gain_gradient,
                second_shift_gradient,
            ]
        ).reshape(-1, local)
        packed[g] = jnp.concatenate(proj_g + out_halves + [vectors], axis=0).astype(BF16)
        for c in range(3):
            grad_inputs = grad_inputs + dot(grads[c], proj[g][c], ((1,), (1,)))
    input_gradient = lax.all_gather(grad_inputs.astype(BF16), "tensor", axis=0, tiled=True)
    rest = reduce_rows(pair_sum(packed[0], packed[1]), size).astype(F32)
    projections_gradient = rest[: 3 * width].reshape(3, width, local)
    halves = width // local
    out_rows = rest[3 * width : 3 * width + halves * local]
    output_weight_gradient = jnp.concatenate(
        [out_rows[i * local : (i + 1) * local] for i in range(halves)], axis=1
    )
    vectors = rest[3 * width + halves * local :].reshape(-1)
    attention_bias_gradient = vectors[: 2 * local].reshape(2, local)
    inner_bias_gradient = vectors[2 * local : 2 * local + hidden]
    shared = vectors[2 * local + hidden :].reshape(6, width)
    return (
        layer_output,
        input_gradient,
        projections_gradient,
        attention_bias_gradient,
        output_weight_gradient,
        shared[0],
        shared[1],
        shared[2],
        inner_weight_gradient,
        inner_bias_gradient,
        outer_weight_gradient,
        shared[3],
        shared[4],
        shared[5],
    )


def solution(mesh):
    in_specs = (
        P("dp", None),
        P("dp"),
        P(None, None, "tensor"),
        P(None, "tensor"),
        P("tensor", None),
        P(),
        P(),
        P(),
        P(None, "tensor"),
        P("tensor"),
        P("tensor", None),
        P(),
        P(),
        P(),
        P("dp", None),
    )
    out_specs = (
        P("dp", None),
        P("dp", None),
        P(None, None, "tensor"),
        P(None, "tensor"),
        P("tensor", None),
        P(),
        P(),
        P(),
        P(None, "tensor"),
        P("tensor"),
        P("tensor", None),
        P(),
        P(),
        P(),
    )
    return jax.shard_map(
        functools.partial(per_device, mesh.shape["dp"]),
        mesh=mesh,
        in_specs=in_specs,
        out_specs=out_specs,
        check_vma=False,
    )
```
